32 devices in a mesh: seq: 8 (over z, y), tp: 4 (over x, core).
Axes of the slice: x: 2, y: 2, z: 4, core: 2. Of those that a mesh axis runs over, the one named last changes fastest.
Arguments:
- patches: bfloat16 [4096, 1664], P('seq', 'tp'), may hold values from -30 to 30
- grad_merged: bfloat16 [1024, 1664], P('seq', 'tp'), may hold values from -6 to 6
- norm_gain: float32 [1664], replicated, may hold values from 0.25 to 1.75
- qkv_weight: bfloat16 [1664, 2496], P(None, 'tp'), may hold values from -0.15625 to 0.15625
- proj_weight: bfloat16 [832, 1664], P('tp'), may hold values from -0.21875 to 0.21875
- grid_height: int32 [24], replicated, may hold values from 4 to 8
- grid_width: int32 [24], replicated, may hold values from 3 to 5, as said below
Outputs:
- patch_grad: bfloat16 [4096, 1664], P('seq', 'tp')
- qkv_grad: float32 [1664, 2496], P('seq', 'tp')
The draws below stay inside these ranges and needn't reach their ends.
Inputs may be any that keep to these rules, and one draw needn't show every extreme that they name: `grid_width`: the merged rows of one shard's three images add up to at most 120, exactly that on some shard.
All inputs are finite; a program needn't handle non-finite values.
Results may differ from the reference program's by a relative error of at most 0.011.
Values may be sent and summed in bfloat16 or wider, within the bound.
A program may use at most 64 MiB of HBM per device.

```python
import math
import jax
import jax.numpy as jnp
from jax import lax

D = 1664
HEADS = 8
HEAD_SIZE = 104
MS = 128
GRID_H = 8
IMAGES = 24
GRID_W = 5
TOKENS = 1024
PATCHES = 4096
N_SEQ = 8


def stream_layout(key):
    key_forced, key_height, key_width = jax.random.split(key, 3)
    forced = jax.random.randint(key_forced, (), 0, IMAGES // 3)
    heights = jax.random.randint(key_height, (IMAGES,), GRID_H // 2, GRID_H + 1)
    widths = jax.random.randint(key_width, (IMAGES,), (GRID_W + 1) // 2, GRID_W + 1)
    at_full = jnp.arange(IMAGES) // 3 == forced
    heights = jnp.where(at_full, GRID_H, heights).astype(jnp.int32)
    widths = jnp.where(at_full, GRID_W, widths).astype(jnp.int32)
    return (heights, widths)


def draw_grid_height(key, part):
    shared = stream_layout(key)
    return shared[0]


def draw_grid_width(key, part):
    shared = stream_layout(key)
    return shared[1]


def draw_patches(key, part):
    key = jax.random.fold_in(key, 5)
    key_jitter, key_scale = jax.random.split(key, 2)
    row_scale = jnp.exp(jax.random.uniform(key_scale, (PATCHES, 1), minval=math.log(0.4), maxval=math.log(4.0)))
    values = row_scale * jax.random.normal(key_jitter, (PATCHES, D))
    return values.astype(jnp.float32).astype(jnp.bfloat16)


def levels(key, shape, cuts, smallest, largest):
    loudness = 1.0
    for dim, shards_of in cuts:
        steps = jax.random.uniform(jax.random.fold_in(jax.random.fold_in(key, 6), dim), (shards_of,), jnp.float32, smallest / len(cuts), largest / len(cuts))
        loudness = loudness * jnp.repeat(jnp.exp(steps), shape[dim] // shards_of).reshape((-1,) + (1,) * (len(shape) - 1 - dim))
    return loudness


def normal_values(stream_key, extent, width, bound, cuts=(), kind=jnp.bfloat16):
    entries = width * jax.random.normal(stream_key, extent, jnp.float32)
    if cuts:
        entries = entries * levels(stream_key, extent, cuts, -0.22, 0.18)
    return jnp.clip(entries, -bound, bound).astype(kind)


def setup_inputs(seed: int = 0) -> dict:
    key_of = jax.random.split(jax.random.key(seed), 8)
    return {
        "patches": draw_patches(jax.random.fold_in(key_of[7], 71), 0),
        "grad_merged": normal_values(key_of[1], (TOKENS, D), 1.0, 6.0, ((0, 8), (1, 4))),
        "norm_gain": jnp.clip(1.0 + 0.15 * jax.random.normal(key_of[2], (D,), jnp.float32), 0.25, 1.75),
        "qkv_weight": normal_values(key_of[3], (D, 3 * HEADS * HEAD_SIZE), D ** -0.5, 0.15625, ((1, 4),)),
        "proj_weight": normal_values(key_of[4], (HEADS * HEAD_SIZE, D), (HEADS * HEAD_SIZE) ** -0.5, 0.21875, ((0, 4),)),
        "grid_height": draw_grid_height(jax.random.fold_in(key_of[7], 71), 0),
        "grid_width": draw_grid_width(jax.random.fold_in(key_of[7], 71), 0),
    }


soft_cap = 5.0
norm_eps = 1e-06

def rounded(values):
    return lax.optimization_barrier(values.astype(jnp.bfloat16)).astype(jnp.float32)

def stream_bounds(grid_height, grid_width, shard_count):
    image_sizes = (grid_height * grid_width).astype(jnp.int32)
    image_ends = jnp.cumsum(image_sizes).astype(jnp.int32)
    image_shard = (jnp.arange(image_sizes.shape[0], dtype=jnp.int32) // 3).astype(jnp.int32)
    owner_ids = jnp.arange(shard_count, dtype=jnp.int32)
    shard_load = lax.optimization_barrier(jnp.sum(jnp.where(image_shard[None, :] == owner_ids[:, None], image_sizes[None, :], 0), axis=1)).astype(jnp.int32)
    first_row = lax.optimization_barrier(jnp.sum(jnp.where(image_shard[None, :] < owner_ids[:, None], image_sizes[None, :], 0), axis=1)).astype(jnp.int32)
    return (image_ends, first_row, shard_load)

def block_grads(rows_in, grad_in, image_key, norm_gain, qkv_weight, proj_weight):
    row_total = rows_in.shape[0]
    head_count = qkv_weight.shape[1] // (3 * HEAD_SIZE)
    live = image_key >= 0
    row_values = rows_in.astype(jnp.float32)
    inv_rms = lax.rsqrt(lax.optimization_barrier(jnp.mean(row_values * row_values, axis=-1, keepdims=True)) + norm_eps)
    unit_rows = row_values * inv_rms
    normed = (unit_rows * norm_gain).astype(jnp.bfloat16)
    packed = rounded(jnp.dot(normed, qkv_weight, preferred_element_type=jnp.float32))
    packed = packed.reshape(row_total, head_count, 3, HEAD_SIZE)
    queries = packed[:, :, 0]
    key_rows = packed[:, :, 1]
    values = packed[:, :, 2]
    score_scale = HEAD_SIZE ** (-0.5)
    logits = jnp.einsum('qhe,khe->hqk', queries, key_rows) * score_scale
    capped = jnp.tanh(logits * (1.0 / soft_cap))
    same_image = image_key[:, None] == image_key[None, :]
    raised = jnp.where(same_image[None], jnp.exp(soft_cap * capped), 0.0)
    attn_probs = raised / lax.optimization_barrier(jnp.sum(raised, axis=-1, keepdims=True))
    probs_half = rounded(attn_probs)
    grad_heads = rounded(jnp.dot(grad_in, proj_weight.T, preferred_element_type=jnp.float32))
    grad_heads = grad_heads.reshape(row_total, head_count, HEAD_SIZE)
    grad_prob = jnp.einsum('qhe,khe->hqk', grad_heads, values)
    grad_score = attn_probs * (grad_prob - lax.optimization_barrier(jnp.sum(attn_probs * grad_prob, axis=-1, keepdims=True)))
    grad_logit = rounded(grad_score * (1.0 - capped * capped))
    grad_query = (jnp.einsum('hqk,khe->qhe', grad_logit, key_rows) * score_scale).astype(jnp.bfloat16)
    grad_key = (jnp.einsum('hqk,qhe->khe', grad_logit, queries) * score_scale).astype(jnp.bfloat16)
    grad_value = jnp.einsum('hqk,qhe->khe', probs_half, grad_heads).astype(jnp.bfloat16)
    grad_cols = jnp.stack([grad_query, grad_key, grad_value], axis=2).reshape(row_total, 3 * head_count * HEAD_SIZE)
    grad_normed = jnp.dot(grad_cols, qkv_weight.T, preferred_element_type=jnp.float32)
    scaled = grad_normed * norm_gain
    grad_rows = inv_rms * (scaled - unit_rows * lax.optimization_barrier(jnp.mean(scaled * unit_rows, axis=-1, keepdims=True))) + grad_in.astype(jnp.float32)
    grad_rows = jnp.where(live[:, None], grad_rows, 0.0).astype(jnp.bfloat16)
    return (grad_rows, grad_cols, normed)

def reference(patches, grad_merged, norm_gain, qkv_weight, proj_weight, grid_height, grid_width):
    image_ends, first_row, shard_load = stream_bounds(grid_height, grid_width, N_SEQ)
    merged = (patches.astype(jnp.float32).reshape(TOKENS, 4, D).sum(axis=1) * 0.25).astype(jnp.bfloat16)

    def per_shard(weight_sum, shard):
        local_rows = jnp.arange(MS, dtype=jnp.int32)
        stream_rows = first_row[shard] + local_rows
        live = local_rows < shard_load[shard]
        flat = jnp.where(live, stream_rows % N_SEQ * MS + stream_rows // N_SEQ, 0).astype(jnp.int32)
        rows_in = jnp.where(live[:, None], merged[flat], 0.0).astype(jnp.bfloat16)
        grad_in = jnp.where(live[:, None], grad_merged[flat], 0.0).astype(jnp.bfloat16)
        image_index = lax.optimization_barrier(jnp.sum(image_ends[None, :] <= stream_rows[:, None], axis=1)).astype(jnp.int32)
        image_key = jnp.where(live, image_index, -1 - local_rows).astype(jnp.int32)
        grad_rows, grad_cols, normed = block_grads(rows_in, grad_in, image_key, norm_gain, qkv_weight, proj_weight)
        weight_sum = weight_sum + jnp.dot(normed.T, grad_cols, preferred_element_type=jnp.float32)
        target = jnp.where(live, flat, TOKENS).astype(jnp.int32)
        return (weight_sum, (grad_rows, target))
    start_sum = jnp.zeros((D, 3 * HEADS * HEAD_SIZE), jnp.float32)
    weight_sum, (grad_all, target_all) = lax.scan(per_shard, start_sum, jnp.arange(N_SEQ, dtype=jnp.int32))
    grad_source = jnp.zeros((TOKENS, D), jnp.bfloat16).at[target_all.reshape(-1)].set(grad_all.reshape(-1, D), mode='drop')
    patch_grad = jnp.broadcast_to((grad_source * 0.25)[:, None, :], (TOKENS, 4, D)).reshape(PATCHES, D)
    qkv_grad = weight_sum * TOKENS ** (-0.5)
    return (patch_grad, qkv_grad)
```

```python
import functools

import jax
import jax.numpy as jnp
from jax import lax
from jax.experimental import pallas as pl
from jax.experimental.pallas import tpu as pltpu
from jax.sharding import PartitionSpec as P

HEAD_SIZE = 104


soft_cap = 5.0
norm_eps = 1e-06


def stream_bounds(grid_height, grid_width, shard_count):
    image_sizes = grid_height * grid_width
    image_ends = jnp.cumsum(image_sizes)
    image_shard = jnp.arange(image_sizes.shape[0], dtype=jnp.int32) // 3
    owner_ids = jnp.arange(shard_count, dtype=jnp.int32)
    shard_load = jnp.sum(
        jnp.where(image_shard[None, :] == owner_ids[:, None], image_sizes[None, :], 0), axis=1
    )
    first_row = jnp.sum(
        jnp.where(image_shard[None, :] < owner_ids[:, None], image_sizes[None, :], 0), axis=1
    )
    return (image_ends, first_row, shard_load)


def pooled(window_rows, feat_width):
    summed = window_rows.reshape(-1, 4, feat_width).astype(jnp.float32).sum(axis=1)
    return (summed * 0.25).astype(jnp.bfloat16)


def on_device(patches, grad_merged, norm_gain, qkv_weight, proj_weight, grid_height, grid_width):
    shard_count = lax.axis_size("seq")
    myself = lax.axis_index("seq")
    tp_index = lax.axis_index("tp")
    row_count = grad_merged.shape[0]
    feat_width = grad_merged.shape[1]
    slot_count = -(-row_count // shard_count)
    slot_total = shard_count * slot_count
    image_ends, first_row, shard_load = stream_bounds(grid_height, grid_width, shard_count)
    stream_total = image_ends[-1]
    slot_ids = jnp.arange(slot_count, dtype=jnp.int32)
    owner_ids = jnp.arange(shard_count, dtype=jnp.int32)
    lead_row = (first_row - myself + shard_count - 1) // shard_count
    placed = lead_row[:, None] + slot_ids[None, :]
    sending = (placed * shard_count + myself < (first_row + shard_load)[:, None]) & (
        placed < row_count
    )
    picked = jnp.minimum(placed, row_count - 1).reshape(-1)

    def outgoing(source_rows):
        chosen = source_rows[picked].reshape(shard_count, slot_count, source_rows.shape[1])
        return jnp.where(sending[:, :, None], chosen, 0)

    windows = patches.reshape(row_count, 4 * feat_width)
    arrived_win, arrived_grad = (
        lax.all_to_all(outgoing(windows), "seq", split_axis=0, concat_axis=0, tiled=True),
        lax.all_to_all(outgoing(grad_merged), "seq", split_axis=0, concat_axis=0, tiled=True),
    )
    arrived = pooled(arrived_win.reshape(slot_total, 4 * feat_width), feat_width)
    arrived_grad = arrived_grad.reshape(slot_total, feat_width)
    row_values, row_grads = (
        lax.all_gather(arrived, "tp", axis=1, tiled=True),
        lax.all_gather(arrived_grad, "tp", axis=1, tiled=True),
    )
    first_here = first_row[myself]
    end_here = first_here + shard_load[myself]
    stream_in = (
        ((first_here - owner_ids + shard_count - 1) // shard_count)[:, None] + slot_ids[None, :]
    ) * shard_count + owner_ids[:, None]
    stream_in = stream_in.reshape(-1)
    live = stream_in < end_here
    image_index = jnp.sum(image_ends[None, :] <= stream_in[:, None], axis=1)
    image_key = jnp.where(live, image_index, -1 - jnp.arange(slot_total, dtype=jnp.int32))
    same_image = image_key[:, None] == image_key[None, :]
    values_f32 = row_values.astype(jnp.float32)
    inv_rms = lax.rsqrt(jnp.mean(values_f32 * values_f32, axis=-1, keepdims=True) + norm_eps)
    unit_rows = values_f32 * inv_rms
    normed = (unit_rows * norm_gain).astype(jnp.bfloat16)
    head_count = qkv_weight.shape[1] // (3 * HEAD_SIZE)
    packed = jnp.dot(normed, qkv_weight, preferred_element_type=jnp.float32).astype(jnp.bfloat16)
    packed = packed.reshape(slot_total, head_count, 3, HEAD_SIZE)
    queries = packed[:, :, 0]
    key_rows = packed[:, :, 1]
    values = packed[:, :, 2]
    score_scale = HEAD_SIZE ** (-0.5)
    logits = (
        jnp.einsum("qhe,khe->hqk", queries, key_rows, preferred_element_type=jnp.float32)
        * score_scale
    )
    capped = jnp.tanh(logits * (1.0 / soft_cap))
    raised = jnp.where(same_image[None], jnp.exp(soft_cap * capped), 0.0)
    attn_probs = raised / jnp.sum(raised, axis=-1, keepdims=True)
    probs_half = attn_probs.astype(jnp.bfloat16)
    grad_heads = jnp.einsum(
        "rd,cd->rc", row_grads, proj_weight, preferred_element_type=jnp.float32
    ).astype(jnp.bfloat16)
    grad_heads = grad_heads.reshape(slot_total, head_count, HEAD_SIZE)
    grad_prob = jnp.einsum("qhe,khe->hqk", grad_heads, values, preferred_element_type=jnp.float32)
    grad_score = attn_probs * (grad_prob - jnp.sum(attn_probs * grad_prob, axis=-1, keepdims=True))
    grad_logit = (grad_score * (1.0 - capped * capped)).astype(jnp.bfloat16)
    grad_query = (
        jnp.einsum("hqk,khe->qhe", grad_logit, key_rows, preferred_element_type=jnp.float32)
        * score_scale
    ).astype(jnp.bfloat16)
    grad_key = (
        jnp.einsum("hqk,qhe->khe", grad_logit, queries, preferred_element_type=jnp.float32)
        * score_scale
    ).astype(jnp.bfloat16)
    grad_value = jnp.einsum(
        "hqk,qhe->khe", probs_half, grad_heads, preferred_element_type=jnp.float32
    ).astype(jnp.bfloat16)
    grad_cols = jnp.stack([grad_query, grad_key, grad_value], axis=2).reshape(
        slot_total, 3 * head_count * HEAD_SIZE
    )
    head_part = jnp.einsum("rc,dc->rd", grad_cols, qkv_weight, preferred_element_type=jnp.float32)
    grad_normed = lax.psum(head_part, "tp")
    scaled = grad_normed * norm_gain
    grad_rows = inv_rms * (
        scaled - unit_rows * jnp.mean(scaled * unit_rows, axis=-1, keepdims=True)
    ) + row_grads.astype(jnp.float32)
    grad_rows = jnp.where(live[:, None], grad_rows, 0.0).astype(jnp.bfloat16)
    own_cols = lax.dynamic_slice_in_dim(grad_rows, tp_index * feat_width, feat_width, 1)
    local_rows = jnp.arange(row_count, dtype=jnp.int32)
    stream_out = local_rows * shard_count + myself
    owner_of = jnp.sum((first_row + shard_load)[None, :] <= stream_out[:, None], axis=1)
    owner_safe = jnp.minimum(owner_of, shard_count - 1)
    valid_out = stream_out < stream_total
    flat_out = jnp.clip(
        owner_safe * slot_count + local_rows - lead_row[owner_safe], 0, slot_total - 1
    )
    quarter = jnp.broadcast_to((own_cols * 0.25)[:, None, :], (slot_total, 4, feat_width))
    returned = lax.all_to_all(
        quarter.reshape(shard_count, slot_count, 4 * feat_width),
        "seq",
        split_axis=0,
        concat_axis=0,
        tiled=True,
    )
    windows_back = returned.reshape(slot_total, 4 * feat_width)[flat_out]
    windows_back = jnp.where(valid_out[:, None], windows_back, 0)
    patch_grad = windows_back.reshape(4 * row_count, feat_width)
    qkv_sum = lax.psum_scatter(
        jnp.einsum("rd,rc->dc", normed, grad_cols, preferred_element_type=jnp.float32),
        "seq",
        scatter_dimension=0,
        tiled=True,
    )
    qkv_grad = qkv_sum * (row_count * shard_count) ** (-0.5)
    return (patch_grad, qkv_grad)


MESH = pl.DeviceIdType.MESH
NT = (((1,), (1,)), ((), ()))
TN = (((0,), (0,)), ((), ()))
BF = jnp.bfloat16
F32 = jnp.float32


def mm(a, b, dims=(((1,), (0,)), ((), ()))):
    return lax.dot_general(a, b, dims, preferred_element_type=F32)


def kernel(
    S,
    T,
    gh_ref,
    gw_ref,
    gain_ref,
    patches_hbm,
    grads_hbm,
    w_hbm,
    proj_hbm,
    pg_ref,
    qg_ref,
    patches,
    grads,
    w,
    proj,
    picked,
    xg,
    nrm,
    nrmf,
    nst,
    nall,
    gcall,
    hps,
    hpr,
    outr,
    ret,
    load_sem,
    s1s,
    s1r,
    s2s,
    s2r,
    n1s,
    n1r,
    n2s,
    n2r,
    gzs,
    gzr,
    gys,
    gyr,
    hs,
    hr,
    rs,
    rr,
):
    s = lax.axis_index("seq")
    t = lax.axis_index("tp")
    rows = grads.shape[0]
    feat = grads.shape[1]
    slot = rows // S
    quart = rows // T
    wide = T * feat
    nslice = wide // S
    per_block = S // T
    Z = S // 2
    z = s // 2
    y = lax.rem(s, 2)
    t_core = t + 1 - 2 * lax.rem(t, 2)
    t_x = lax.rem(t + 2, T)
    t_far = t_core + 2 - 4 * (t_core // 2)
    s_y = s + 1 - 2 * y

    loads = [
        pltpu.make_async_copy(a, b, load_sem.at[i])
        for i, (a, b) in enumerate(
            ((patches_hbm, patches), (grads_hbm, grads), (w_hbm, w), (proj_hbm, proj))
        )
    ]
    for c in loads:
        c.start()

    def seq_peer(k):
        return lax.rem(s + k, S)

    def seq_from(k):
        return lax.rem(s + S - k, S)

    barrier = pltpu.get_barrier_semaphore()
    for k in range(1, S):
        pl.semaphore_signal(barrier, inc=1, device_id=(seq_peer(k), t), device_id_type=MESH)
    for k in range(1, T):
        pl.semaphore_signal(barrier, inc=1, device_id=(s, lax.rem(t + k, T)), device_id_type=MESH)

    starts = []
    total = jnp.int32(0)
    first_here = jnp.int32(0)
    sizes = []
    for i in range(3 * S):
        if i % 3 == 0:
            starts.append(total)
            first_here = jnp.where(s == i // 3, total, first_here)
        size = gh_ref[i] * gw_ref[i]
        sizes.append(size)
        total = total + size
    starts.append(total)
    end0 = first_here
    end1 = first_here
    end2 = first_here
    for d in range(S):
        here = s == d
        end0 = jnp.where(here, starts[d] + sizes[3 * d], end0)
        end1 = jnp.where(here, starts[d] + sizes[3 * d] + sizes[3 * d + 1], end1)
        end2 = jnp.where(here, starts[d + 1], end2)

    def local_row(shape, dim):
        r = lax.broadcasted_iota(jnp.int32, shape, dim)
        d_of = r // slot
        j = r - d_of * slot
        lead = jnp.zeros(shape, jnp.int32)
        end = jnp.zeros(shape, jnp.int32)
        for d in range(S):
            lead = jnp.where(d_of == d, (starts[d] - s + S - 1) // S, lead)
            end = jnp.where(d_of == d, starts[d + 1], end)
        row = lead + j
        return jnp.where((row * S + s < end) & (row < rows), row, -1)

    def arrival(shape, dim):
        r = lax.broadcasted_iota(jnp.int32, shape, dim)
        o = r // slot
        j = r - o * slot
        g = ((first_here - o + S - 1) // S + j) * S + o
        alive = g < end2
        key = jnp.where(g >= end0, 1, 0) + jnp.where(g >= end1, 1, 0)
        return jnp.where(alive, key, 3 + r), alive

    lrow = local_row((rows, 1), 0)
    sel4 = jnp.where(
        lax.broadcasted_iota(jnp.int32, (rows, 4 * rows), 1) // 4 == lrow, 0.25, 0.0
    ).astype(BF)
    sel1 = jnp.where(lax.broadcasted_iota(jnp.int32, (rows, rows), 1) == lrow, 1.0, 0.0).astype(BF)
    loads[0].wait()
    picked[0] = mm(sel4, patches[...]).astype(BF)
    loads[1].wait()
    picked[1] = mm(sel1, grads[...]).astype(BF)

    pl.semaphore_wait(barrier, S + T - 2)

    def rc(src, dst, ss, rsem, dev):
        return pltpu.make_async_remote_copy(
            src_ref=src,
            dst_ref=dst,
            send_sem=ss,
            recv_sem=rsem,
            device_id=dev,
            device_id_type=MESH,
        )

    def rows_at(i, n):
        return pl.ds(pl.multiple_of(i * n, n), n)

    pending = []

    def send(*a):
        c = rc(*a)
        c.start()
        pending.append(c)

    for k in range(1, S):
        d = seq_peer(k)
        send(
            picked.at[:, rows_at(d, slot), :],
            xg.at[t, :, rows_at(s, slot), :],
            s1s.at[k],
            s1r.at[k],
            (d, t),
        )
    xg[t, :, rows_at(s, slot), :] = picked[:, rows_at(s, slot), :]
    key_r, live = arrival((rows, 1), 0)
    key_c, _ = arrival((1, rows), 1)
    same = key_r == key_c
    for k in range(1, S):
        o = seq_from(k)
        rc(
            picked.at[:, rows_at(o, slot), :],
            xg.at[t, :, rows_at(o, slot), :],
            s1s.at[k],
            s1r.at[k],
            (o, t),
        ).wait_recv()
    for i in range(2):
        send(xg.at[t, i], xg.at[t, i], s2s.at[0, i], s2r.at[0, i], (s, t_x))
        send(xg.at[t, i], xg.at[t, i], s2s.at[1, i], s2r.at[1, i], (s, t_core))
    for i in range(2):
        rc(xg.at[t_x, i], xg.at[t_x, i], s2s.at[0, i], s2r.at[0, i], (s, t_x)).wait_recv()
        send(xg.at[t_x, i], xg.at[t_x, i], s2s.at[2, i], s2r.at[2, i], (s, t_core))

    def wait_rest(i):
        rc(xg.at[t_core, i], xg.at[t_core, i], s2s.at[1, i], s2r.at[1, i], (s, t_core)).wait_recv()
        rc(xg.at[t_far, i], xg.at[t_far, i], s2s.at[2, i], s2r.at[2, i], (s, t_core)).wait_recv()

    wait_rest(0)
    square = jnp.zeros((rows, 1), F32)
    for b in range(T):
        v = xg[b, 0].astype(F32)
        square = square + jnp.sum(v * v, axis=1, keepdims=True)
    inv = lax.rsqrt(square * (1.0 / wide) + norm_eps)
    for b in range(T):
        v = xg[b, 0].astype(F32) * inv * gain_ref[b]
        nrm[b] = v.astype(BF)
        nrmf[b] = v
    for d in range(S):
        off = (d % per_block) * nslice
        part = nrmf[d // per_block, rows_at(t, quart), :]
        nst[d] = part[:, off : off + nslice].astype(BF)
    for k in range(1, S):
        d = seq_peer(k)
        send(nst.at[d], nall.at[s, rows_at(t, quart), :], n1s.at[k], n1r.at[k], (d, t))
    nall[s, rows_at(t, quart), :] = nst[s]

    loads[2].wait()
    packed = jnp.zeros((rows, w.shape[1]), F32)
    for b in range(T):
        packed = packed + mm(nrm[b], w[b * feat : (b + 1) * feat, :])
    loads[3].wait()
    wait_rest(1)
    heads_grad = jnp.zeros((rows, proj.shape[0]), F32)
    for b in range(T):
        heads_grad = heads_grad + mm(xg[b, 1], proj[:, b * feat : (b + 1) * feat], NT)

    head_count = w.shape[1] // (3 * HEAD_SIZE)
    scale = HEAD_SIZE ** (-0.5)
    cols = []
    for h in range(head_count):
        q, kk, v = (
            packed[:, (3 * h + i) * HEAD_SIZE : (3 * h + i + 1) * HEAD_SIZE].astype(BF)
            for i in range(3)
        )
        gh = heads_grad[:, h * HEAD_SIZE : (h + 1) * HEAD_SIZE].astype(BF)
        capped = jnp.tanh(mm(q, kk, NT) * (scale / soft_cap))
        raised = jnp.where(same, jnp.exp(soft_cap * capped), 0.0)
        prob = raised / jnp.sum(raised, axis=1, keepdims=True)
        gp = mm(gh, v, NT)
        gs = prob * (gp - jnp.sum(prob * gp, axis=1, keepdims=True))
        gl = (gs * (1.0 - capped * capped)).astype(BF)
        cols.append(mm(gl, kk) * scale)
        cols.append(mm(gl, q, TN) * scale)
        cols.append(mm(prob.astype(BF), gh, TN))
    grad_f = jnp.concatenate(cols, axis=1)
    grad_cols = grad_f.astype(BF)
    gcall[s] = grad_cols
    for k in range(1, Z):
        send(gcall.at[s], gcall.at[s], gzs.at[k], gzr.at[k], (2 * lax.rem(z + k, Z) + y, t))
    send(gcall.at[s], gcall.at[s], gys.at[0], gyr.at[0], (s_y, t))

    row_dot = jnp.sum(grad_cols.astype(F32) * packed, axis=1, keepdims=True)
    lanes = hps.shape[2]
    dot_tile = jnp.broadcast_to(row_dot, (rows, lanes - feat))

    def head_part(b):
        part = mm(grad_cols, w[pl.ds(pl.multiple_of(b * feat, 16), feat), :], NT)
        return jnp.concatenate([part, dot_tile], axis=1)

    for i, b in enumerate((t_x, t_far, t_core)):
        hps[i] = head_part(b).astype(BF)
        send(hps.at[i], hpr.at[i], hs.at[i], hr.at[i], (s, b))
    own_part = head_part(t)

    for k in range(1, S):
        o = seq_from(k)
        rc(nst.at[o], nall.at[o, rows_at(t, quart), :], n1s.at[k], n1r.at[k], (o, t)).wait_recv()

    def nq(b):
        return nall.at[:, rows_at(b, quart), :]

    send(nq(t), nq(t), n2s.at[0], n2r.at[0], (s, t_x))
    send(nq(t), nq(t), n2s.at[1], n2r.at[1], (s, t_core))

    def forward(k):
        src = 2 * lax.rem(z + Z - k, Z) + y
        rc(gcall.at[src], gcall.at[src], gzs.at[k], gzr.at[k], (src, t)).wait_recv()
        send(gcall.at[src], gcall.at[src], gys.at[k], gyr.at[k], (s_y, t))

    for i, b in enumerate((t_x, t_far, t_core)):
        rc(hps.at[i], hpr.at[i], hs.at[i], hr.at[i], (s, b)).wait_recv()
        own_part = own_part + hpr[i].astype(F32)
    scaled = own_part[:, :feat] * gain_ref[t]
    mean = own_part[:, feat : feat + 1] * (1.0 / wide)
    unit = xg[t, 0].astype(F32) * inv
    grad_rows = inv * (scaled - unit * mean) + xg[t, 1].astype(F32)
    outr[...] = jnp.where(live, grad_rows, 0.0).astype(BF)
    for k in range(1, S):
        d = seq_peer(k)
        send(
            outr.at[rows_at(d, slot), :], ret.at[rows_at(s, slot), :], rs.at[k], rr.at[k], (d, t)
        )
    ret[rows_at(s, slot), :] = outr[rows_at(s, slot), :]

    rc(nq(t_x), nq(t_x), n2s.at[0], n2r.at[0], (s, t_x)).wait_recv()
    send(nq(t_x), nq(t_x), n2s.at[2], n2r.at[2], (s, t_core))
    for k in range(1, Z):
        forward(k)

    lcol = local_row((1, rows), 1)
    back = jnp.where(
        lax.broadcasted_iota(jnp.int32, (4 * rows, rows), 0) // 4 == lcol, 0.25, 0.0
    ).astype(BF)
    for k in range(1, S):
        o = seq_from(k)
        rc(
            outr.at[rows_at(o, slot), :], ret.at[rows_at(o, slot), :], rs.at[k], rr.at[k], (o, t)
        ).wait_recv()
    pg_ref[...] = mm(back, ret[...]).astype(BF)

    rc(nq(t_core), nq(t_core), n2s.at[1], n2r.at[1], (s, t_core)).wait_recv()
    rc(nq(t_far), nq(t_far), n2s.at[2], n2r.at[2], (s, t_core)).wait_recv()

    for k in range(Z):
        src = 2 * lax.rem(z + Z - k, Z) + 1 - y
        rc(gcall.at[src], gcall.at[src], gys.at[k], gyr.at[k], (s_y, t)).wait_recv()
    acc = jnp.zeros(qg_ref.shape, F32)
    for o in range(S):
        acc = acc + mm(nall[o], gcall[o], TN)
    qg_ref[...] = acc * (rows * S) ** (-0.5)
    for c in pending:
        c.wait_send()


def fused(S, T, patches, grad_merged, norm_gain, qkv_weight, proj_weight, grid_height, grid_width):
    rows, feat = grad_merged.shape
    cols = qkv_weight.shape[1]
    slot = rows // S
    quart = rows // T
    nslice = T * feat // S
    lanes = feat // 128 * 128 + 128
    Z = S // 2
    vm, sem = pltpu.VMEM, pltpu.SemaphoreType.DMA
    return pl.pallas_call(
        functools.partial(kernel, S, T),
        out_shape=(
            jax.ShapeDtypeStruct(patches.shape, BF),
            jax.ShapeDtypeStruct((nslice, cols), F32),
        ),
        in_specs=[pl.BlockSpec(memory_space=pltpu.SMEM)] * 2
        + [pl.BlockSpec(memory_space=pltpu.VMEM)]
        + [pl.BlockSpec(memory_space=pl.ANY)] * 4,
        out_specs=[pl.BlockSpec(memory_space=pltpu.VMEM)] * 2,
        scratch_shapes=[
            vm(patches.shape, BF),
            vm((rows, feat), BF),
            vm(qkv_weight.shape, BF),
            vm(proj_weight.shape, BF),
            vm((2, rows, feat), BF),
            vm((T, 2, rows, feat), BF),
            vm((T, rows, feat), BF),
            vm((T, rows, feat), F32),
            vm((S, quart, nslice), BF),
            vm((S, rows, nslice), BF),
            vm((S, rows, cols), BF),
            vm((T - 1, rows, lanes), BF),
            vm((T - 1, rows, lanes), BF),
            vm((rows, feat), BF),
            vm((rows, feat), BF),
            sem((4,)),
            sem((S,)),
            sem((S,)),
            sem((3, 2)),
            sem((3, 2)),
            sem((S,)),
            sem((S,)),
            sem((3,)),
            sem((3,)),
            sem((Z,)),
            sem((Z,)),
            sem((Z,)),
            sem((Z,)),
            sem((T - 1,)),
            sem((T - 1,)),
            sem((S,)),
            sem((S,)),
        ],
        compiler_params=pltpu.CompilerParams(
            collective_id=0, has_side_effects=True, vmem_limit_bytes=40 * 1024 * 1024
        ),
        cost_estimate=pl.CostEstimate(flops=1 << 30, bytes_accessed=5 << 20, transcendentals=1 << 16),
    )(
        grid_height,
        grid_width,
        norm_gain.reshape(T, 1, feat),
        patches,
        grad_merged,
        qkv_weight,
        proj_weight,
    )


def solution(mesh):
    in_specs = (P("seq", "tp"), P("seq", "tp"), P(), P(None, "tp"), P("tp", None), P(), P())
    out_specs = (P("seq", "tp"), P("seq", "tp"))
    S, T = mesh.shape["seq"], mesh.shape["tp"]

    def body(*args):
        rows = args[1].shape[0]
        slot = rows // S
        if T == 4 and S % 2 == 0 and S <= 16 and rows % S == 0 and slot % 16 == 0:
            return fused(S, T, *args)
        return on_device(*args)

    return jax.shard_map(body, mesh=mesh, in_specs=in_specs, out_specs=out_specs, check_vma=False)
```

```python
import functools

import jax
import jax.numpy as jnp
from jax import lax
from jax.experimental import pallas as pl
from jax.experimental.pallas import tpu as pltpu
from jax.sharding import PartitionSpec as P

HEAD_SIZE = 104


soft_cap = 5.0
norm_eps = 1e-06


def stream_bounds(grid_height, grid_width, shard_count):
    image_sizes = grid_height * grid_width
    image_ends = jnp.cumsum(image_sizes)
    image_shard = jnp.arange(image_sizes.shape[0], dtype=jnp.int32) // 3
    owner_ids = jnp.arange(shard_count, dtype=jnp.int32)
    shard_load = jnp.sum(
        jnp.where(image_shard[None, :] == owner_ids[:, None], image_sizes[None, :], 0), axis=1
    )
    first_row = jnp.sum(
        jnp.where(image_shard[None, :] < owner_ids[:, None], image_sizes[None, :], 0), axis=1
    )
    return (image_ends, first_row, shard_load)


def pooled(window_rows, feat_width):
    summed = window_rows.reshape(-1, 4, feat_width).astype(jnp.float32).sum(axis=1)
    return (summed * 0.25).astype(jnp.bfloat16)


def on_device(patches, grad_merged, norm_gain, qkv_weight, proj_weight, grid_height, grid_width):
    shard_count = lax.axis_size("seq")
    myself = lax.axis_index("seq")
    tp_index = lax.axis_index("tp")
    row_count = grad_merged.shape[0]
    feat_width = grad_merged.shape[1]
    slot_count = -(-row_count // shard_count)
    slot_total = shard_count * slot_count
    image_ends, first_row, shard_load = stream_bounds(grid_height, grid_width, shard_count)
    stream_total = image_ends[-1]
    slot_ids = jnp.arange(slot_count, dtype=jnp.int32)
    owner_ids = jnp.arange(shard_count, dtype=jnp.int32)
    lead_row = (first_row - myself + shard_count - 1) // shard_count
    placed = lead_row[:, None] + slot_ids[None, :]
    sending = (placed * shard_count + myself < (first_row + shard_load)[:, None]) & (
        placed < row_count
    )
    picked = jnp.minimum(placed, row_count - 1).reshape(-1)

    def outgoing(source_rows):
        chosen = source_rows[picked].reshape(shard_count, slot_count, source_rows.shape[1])
        return jnp.where(sending[:, :, None], chosen, 0)

    windows = patches.reshape(row_count, 4 * feat_width)
    arrived_win, arrived_grad = (
        lax.all_to_all(outgoing(windows), "seq", split_axis=0, concat_axis=0, tiled=True),
        lax.all_to_all(outgoing(grad_merged), "seq", split_axis=0, concat_axis=0, tiled=True),
    )
    arrived = pooled(arrived_win.reshape(slot_total, 4 * feat_width), feat_width)
    arrived_grad = arrived_grad.reshape(slot_total, feat_width)
    row_values, row_grads = (
        lax.all_gather(arrived, "tp", axis=1, tiled=True),
        lax.all_gather(arrived_grad, "tp", axis=1, tiled=True),
    )
    first_here = first_row[myself]
    end_here = first_here + shard_load[myself]
    stream_in = (
        ((first_here - owner_ids + shard_count - 1) // shard_count)[:, None] + slot_ids[None, :]
    ) * shard_count + owner_ids[:, None]
    stream_in = stream_in.reshape(-1)
    live = stream_in < end_here
    image_index = jnp.sum(image_ends[None, :] <= stream_in[:, None], axis=1)
    image_key = jnp.where(live, image_index, -1 - jnp.arange(slot_total, dtype=jnp.int32))
    same_image = image_key[:, None] == image_key[None, :]
    values_f32 = row_values.astype(jnp.float32)
    inv_rms = lax.rsqrt(jnp.mean(values_f32 * values_f32, axis=-1, keepdims=True) + norm_eps)
    unit_rows = values_f32 * inv_rms
    normed = (unit_rows * norm_gain).astype(jnp.bfloat16)
    head_count = qkv_weight.shape[1] // (3 * HEAD_SIZE)
    packed = jnp.dot(normed, qkv_weight, preferred_element_type=jnp.float32).astype(jnp.bfloat16)
    packed = packed.reshape(slot_total, head_count, 3, HEAD_SIZE)
    queries = packed[:, :, 0]
    key_rows = packed[:, :, 1]
    values = packed[:, :, 2]
    score_scale = HEAD_SIZE ** (-0.5)
    logits = (
        jnp.einsum("qhe,khe->hqk", queries, key_rows, preferred_element_type=jnp.float32)
        * score_scale
    )
    capped = jnp.tanh(logits * (1.0 / soft_cap))
    raised = jnp.where(same_image[None], jnp.exp(soft_cap * capped), 0.0)
    attn_probs = raised / jnp.sum(raised, axis=-1, keepdims=True)
    probs_half = attn_probs.astype(jnp.bfloat16)
    grad_heads = jnp.einsum(
        "rd,cd->rc", row_grads, proj_weight, preferred_element_type=jnp.float32
    ).astype(jnp.bfloat16)
    grad_heads = grad_heads.reshape(slot_total, head_count, HEAD_SIZE)
    grad_prob = jnp.einsum("qhe,khe->hqk", grad_heads, values, preferred_element_type=jnp.float32)
    grad_score = attn_probs * (grad_prob - jnp.sum(attn_probs * grad_prob, axis=-1, keepdims=True))
    grad_logit = (grad_score * (1.0 - capped * capped)).astype(jnp.bfloat16)
    grad_query = (
        jnp.einsum("hqk,khe->qhe", grad_logit, key_rows, preferred_element_type=jnp.float32)
        * score_scale
    ).astype(jnp.bfloat16)
    grad_key = (
        jnp.einsum("hqk,qhe->khe", grad_logit, queries, preferred_element_type=jnp.float32)
        * score_scale
    ).astype(jnp.bfloat16)
    grad_value = jnp.einsum(
        "hqk,qhe->khe", probs_half, grad_heads, preferred_element_type=jnp.float32
    ).astype(jnp.bfloat16)
    grad_cols = jnp.stack([grad_query, grad_key, grad_value], axis=2).reshape(
        slot_total, 3 * head_count * HEAD_SIZE
    )
    head_part = jnp.einsum("rc,dc->rd", grad_cols, qkv_weight, preferred_element_type=jnp.float32)
    grad_normed = lax.psum(head_part, "tp")
    scaled = grad_normed * norm_gain
    grad_rows = inv_rms * (
        scaled - unit_rows * jnp.mean(scaled * unit_rows, axis=-1, keepdims=True)
    ) + row_grads.astype(jnp.float32)
    grad_rows = jnp.where(live[:, None], grad_rows, 0.0).astype(jnp.bfloat16)
    own_cols = lax.dynamic_slice_in_dim(grad_rows, tp_index * feat_width, feat_width, 1)
    local_rows = jnp.arange(row_count, dtype=jnp.int32)
    stream_out = local_rows * shard_count + myself
    owner_of = jnp.sum((first_row + shard_load)[None, :] <= stream_out[:, None], axis=1)
    owner_safe = jnp.minimum(owner_of, shard_count - 1)
    valid_out = stream_out < stream_total
    flat_out = jnp.clip(
        owner_safe * slot_count + local_rows - lead_row[owner_safe], 0, slot_total - 1
    )
    quarter = jnp.broadcast_to((own_cols * 0.25)[:, None, :], (slot_total, 4, feat_width))
    returned = lax.all_to_all(
        quarter.reshape(shard_count, slot_count, 4 * feat_width),
        "seq",
        split_axis=0,
        concat_axis=0,
        tiled=True,
    )
    windows_back = returned.reshape(slot_total, 4 * feat_width)[flat_out]
    windows_back = jnp.where(valid_out[:, None], windows_back, 0)
    patch_grad = windows_back.reshape(4 * row_count, feat_width)
    qkv_sum = lax.psum_scatter(
        jnp.einsum("rd,rc->dc", normed, grad_cols, preferred_element_type=jnp.float32),
        "seq",
        scatter_dimension=0,
        tiled=True,
    )
    qkv_grad = qkv_sum * (row_count * shard_count) ** (-0.5)
    return (patch_grad, qkv_grad)


MESH = pl.DeviceIdType.MESH
NT = (((1,), (1,)), ((), ()))
TN = (((0,), (0,)), ((), ()))
BF = jnp.bfloat16
F32 = jnp.float32


def mm(a, b, dims=(((1,), (0,)), ((), ()))):
    return lax.dot_general(a, b, dims, preferred_element_type=F32)


def kernel(
    S,
    T,
    gh_ref,
    gw_ref,
    gain_ref,
    patches_hbm,
    grads_hbm,
    w_hbm,
    proj_hbm,
    pg_ref,
    qg_ref,
    patches,
    grads,
    w,
    proj,
    picked,
    xg,
    nrmf,
    nst,
    nall,
    gcall,
    hps,
    hpr,
    outr,
    ret,
    load_sem,
    s1s,
    s1r,
    s2s,
    s2r,
    n1s,
    n1r,
    n2s,
    n2r,
    gzs,
    gzr,
    gys,
    gyr,
    hs,
    hr,
    rs,
    rr,
):
    s = lax.axis_index("seq")
    t = lax.axis_index("tp")
    feat, rows = grads.shape
    half = S // 2
    slot = rows // S
    quart = rows // T
    wide = T * feat
    nslice = wide // S
    per_block = S // T
    Z = S // 2
    z = s // 2
    y = lax.rem(s, 2)
    t_core = t + 1 - 2 * lax.rem(t, 2)
    t_x = lax.rem(t + 2, T)
    t_far = t_core + 2 - 4 * (t_core // 2)
    s_y = s + 1 - 2 * y

    loads = [
        pltpu.make_async_copy(a, b, load_sem.at[i])
        for i, (a, b) in enumerate(
            ((patches_hbm, patches), (grads_hbm, grads), (w_hbm, w), (proj_hbm, proj))
        )
    ]
    for c in loads:
        c.start()

    def seq_peer(k):
        return lax.rem(s + k, S)

    def seq_from(k):
        return lax.rem(s + S - k, S)

    barrier = pltpu.get_barrier_semaphore()
    for k in range(1, S):
        pl.semaphore_signal(barrier, inc=1, device_id=(seq_peer(k), t), device_id_type=MESH)
    for k in range(1, T):
        pl.semaphore_signal(barrier, inc=1, device_id=(s, lax.rem(t + k, T)), device_id_type=MESH)

    starts = []
    total = jnp.int32(0)
    first_here = jnp.int32(0)
    sizes = []
    for i in range(3 * S):
        if i % 3 == 0:
            starts.append(total)
            first_here = jnp.where(s == i // 3, total, first_here)
        size = gh_ref[i] * gw_ref[i]
        sizes.append(size)
        total = total + size
    starts.append(total)
    end0 = first_here
    end1 = first_here
    end2 = first_here
    for d in range(S):
        here = s == d
        end0 = jnp.where(here, starts[d] + sizes[3 * d], end0)
        end1 = jnp.where(here, starts[d] + sizes[3 * d] + sizes[3 * d + 1], end1)
        end2 = jnp.where(here, starts[d + 1], end2)

    def local_row(shape, dim):
        r = lax.broadcasted_iota(jnp.int32, shape, dim)
        d_of = r // slot
        j = r - d_of * slot
        lead = jnp.zeros(shape, jnp.int32)
        end = jnp.zeros(shape, jnp.int32)
        for d in range(S):
            lead = jnp.where(d_of == d, (starts[d] - s + S - 1) // S, lead)
            end = jnp.where(d_of == d, starts[d + 1], end)
        row = lead + j
        return jnp.where((row * S + s < end) & (row < rows), row, -1)

    def arrival(shape, dim):
        r = lax.broadcasted_iota(jnp.int32, shape, dim)
        o = r // slot
        j = r - o * slot
        g = ((first_here - o + S - 1) // S + j) * S + o
        alive = g < end2
        key = jnp.where(g >= end0, 1, 0) + jnp.where(g >= end1, 1, 0)
        return jnp.where(alive, key, 3 + r), alive

    lrow = local_row((rows, 1), 0)
    sel4 = jnp.where(
        lax.broadcasted_iota(jnp.int32, (rows, 4 * rows), 1) // 4 == lrow, 0.25, 0.0
    ).astype(BF)
    sel1 = jnp.where(lax.broadcasted_iota(jnp.int32, (rows, rows), 1) == lrow, 1.0, 0.0).astype(BF)
    loads[0].wait()
    picked[0] = mm(sel4, patches[...], NT).astype(BF)
    loads[1].wait()
    picked[1] = mm(sel1, grads[...], NT).astype(BF)

    pl.semaphore_wait(barrier, S + T - 2)

    def rc(src, dst, ss, rsem, dev):
        return pltpu.make_async_remote_copy(
            src_ref=src,
            dst_ref=dst,
            send_sem=ss,
            recv_sem=rsem,
            device_id=dev,
            device_id_type=MESH,
        )

    def rows_at(i, n):
        return pl.ds(pl.multiple_of(i * n, n), n)

    pending = []

    def send(*a):
        c = rc(*a)
        c.start()
        pending.append(c)

    side = s // half
    place = lax.rem(s, half)

    def group(g):
        return side if g == 0 else 1 - side

    def s1_peer(g, k):
        return group(g) * half + lax.rem(place + k, half)

    def s1_from(g, k):
        return group(g) * half + lax.rem(place + half - k, half)

    def xrows(b, i, g):
        return xg.at[b, i, rows_at(group(g), half * slot), :]

    for i in range(2):
        for g in range(2):
            for k in range(1 - g, half):
                d = s1_peer(g, k)
                send(
                    picked.at[i, rows_at(d, slot), :],
                    xg.at[t, i, rows_at(s, slot), :],
                    s1s.at[i, g * half + k],
                    s1r.at[i, g * half + k],
                    (d, t),
                )
    xg[t, :, rows_at(s, slot), :] = picked[:, rows_at(s, slot), :]
    key_r, live = arrival((rows, 1), 0)
    key_c, _ = arrival((1, rows), 1)
    same = key_r == key_c

    def pass_on(i, g):
        for k in range(1 - g, half):
            o = s1_from(g, k)
            rc(
                picked.at[i, rows_at(o, slot), :],
                xg.at[t, i, rows_at(o, slot), :],
                s1s.at[i, g * half + k],
                s1r.at[i, g * half + k],
                (o, t),
            ).wait_recv()
        send(xrows(t, i, g), xrows(t, i, g), s2s.at[0, i, g], s2r.at[0, i, g], (s, t_x))
        send(xrows(t, i, g), xrows(t, i, g), s2s.at[1, i, g], s2r.at[1, i, g], (s, t_core))

    def relay(i, g):
        block = xrows(t_x, i, g)
        rc(block, block, s2s.at[0, i, g], s2r.at[0, i, g], (s, t_x)).wait_recv()
        send(block, block, s2s.at[2, i, g], s2r.at[2, i, g], (s, t_core))

    def wait_rest(i):
        for g in range(2):
            for j, b in ((1, t_core), (2, t_far)):
                block = xrows(b, i, g)
                rc(block, block, s2s.at[j, i, g], s2r.at[j, i, g], (s, t_core)).wait_recv()

    def all_features(i):
        return jnp.concatenate([xg[b, i].astype(F32) for b in range(T)], axis=1)

    pass_on(0, 0)
    pass_on(0, 1)
    pass_on(1, 0)
    relay(0, 0)
    pass_on(1, 1)
    relay(0, 1)
    wait_rest(0)
    gain = gain_ref[...]
    x_all = all_features(0)
    inv = lax.rsqrt(jnp.sum(x_all * x_all, axis=1, keepdims=True) * (1.0 / wide) + norm_eps)
    normed_f = x_all * inv * gain
    nrmf[...] = normed_f
    normed = normed_f.astype(BF)
    part = nrmf[rows_at(t, quart), :]
    for d in range(S):
        nst[d] = part[:, d * nslice : (d + 1) * nslice].astype(BF)
    for k in range(1, S):
        d = seq_peer(k)
        send(nst.at[d], nall.at[s, rows_at(t, quart), :], n1s.at[k], n1r.at[k], (d, t))
    nall[s, rows_at(t, quart), :] = nst[s]
    relay(1, 0)
    relay(1, 1)

    loads[2].wait()
    packed = mm(normed, w[...], NT)
    loads[3].wait()
    wait_rest(1)
    heads_grad = mm(all_features(1).astype(BF), proj[...], NT)

    head_count = w.shape[0] // (3 * HEAD_SIZE)
    scale = HEAD_SIZE ** (-0.5)
    cols = []
    early = 256
    near = [1, Z - 1] if Z > 2 else [1]
    late = list(range(2, Z - 1))

    def gpart(o, e):
        return gcall.at[o, :, pl.ds(0, early) if e == 0 else pl.ds(early, gcall.shape[2] - early)]

    def z_from(k):
        return 2 * lax.rem(z + Z - k, Z) + y

    def spread(e):
        block = gpart(s, e)
        for k in near + late:
            d = 2 * lax.rem(z + k, Z) + y
            send(block, block, gzs.at[e, k], gzr.at[e, k], (d, t))
        send(block, block, gys.at[e, 0], gyr.at[e, 0], (s_y, t))

    def forward(e, k):
        block = gpart(z_from(k), e)
        rc(block, block, gzs.at[e, k], gzr.at[e, k], (z_from(k), t)).wait_recv()
        send(block, block, gys.at[e, k], gyr.at[e, k], (s_y, t))

    def nq(b):
        return nall.at[:, rows_at(b, quart), :]

    for h in range(head_count):
        q, kk, v = (
            packed[:, (3 * h + i) * HEAD_SIZE : (3 * h + i + 1) * HEAD_SIZE].astype(BF)
            for i in range(3)
        )
        gh = heads_grad[:, h * HEAD_SIZE : (h + 1) * HEAD_SIZE].astype(BF)
        capped = jnp.tanh(mm(q, kk, NT) * (scale / soft_cap))
        raised = jnp.where(same, jnp.exp(soft_cap * capped), 0.0)
        prob = raised / jnp.sum(raised, axis=1, keepdims=True)
        gp = mm(gh, v, NT)
        gs = prob * (gp - jnp.sum(prob * gp, axis=1, keepdims=True))
        gl = (gs * (1.0 - capped * capped)).astype(BF)
        cols.append(mm(gl, kk) * scale)
        cols.append(mm(gl, q, TN) * scale)
        cols.append(mm(prob.astype(BF), gh, TN))
        if h == 0:
            gcall[s, :, :early] = jnp.concatenate(cols, axis=1)[:, :early].astype(BF)
            spread(0)
            for k in range(1, S):
                o = seq_from(k)
                rc(
                    nst.at[o], nall.at[o, rows_at(t, quart), :], n1s.at[k], n1r.at[k], (o, t)
                ).wait_recv()
            send(nq(t), nq(t), n2s.at[0], n2r.at[0], (s, t_x))
            send(nq(t), nq(t), n2s.at[1], n2r.at[1], (s, t_core))
    grad_f = jnp.concatenate(cols, axis=1)
    grad_cols = grad_f.astype(BF)
    spare = gcall.shape[2] - grad_f.shape[1]
    padded = jnp.concatenate([grad_f, jnp.zeros((rows, spare), F32)], axis=1) if spare else grad_f
    gcall[s, :, early:] = padded[:, early:].astype(BF)
    spread(1)

    row_dot = jnp.sum(grad_cols.astype(F32) * packed, axis=1, keepdims=True)
    dot_tile = jnp.broadcast_to(row_dot, (rows, hps.shape[2] - feat))
    every = mm(grad_cols, w[...])
    own_part = jnp.zeros((rows, feat), F32)
    gain_own = jnp.zeros((1, feat), F32)
    for b in range(T):
        part = every[:, b * feat : (b + 1) * feat]
        hps[b] = jnp.concatenate([part, dot_tile], axis=1).astype(BF)
        own_part = jnp.where(t == b, part, own_part)
        gain_own = jnp.where(t == b, gain[:, b * feat : (b + 1) * feat], gain_own)
    for i, b in enumerate((t_x, t_far, t_core)):
        send(hps.at[b], hpr.at[i], hs.at[i], hr.at[i], (s, b))

    rc(nq(t_x), nq(t_x), n2s.at[0], n2r.at[0], (s, t_x)).wait_recv()
    send(nq(t_x), nq(t_x), n2s.at[2], n2r.at[2], (s, t_core))
    for k in near:
        forward(0, k)

    for i, b in enumerate((t_x, t_far, t_core)):
        rc(hps.at[b], hpr.at[i], hs.at[i], hr.at[i], (s, b)).wait_recv()
        came = hpr[i].astype(F32)
        own_part = own_part + came[:, :feat]
        row_dot = row_dot + came[:, feat : feat + 1]
    scaled = own_part * gain_own
    mean = row_dot * (1.0 / wide)
    unit = xg[t, 0].astype(F32) * inv
    grad_rows = inv * (scaled - unit * mean) + xg[t, 1].astype(F32)
    outr[...] = jnp.where(live, grad_rows, 0.0).astype(BF)
    for k in range(1, S):
        d = seq_peer(k)
        send(
            outr.at[rows_at(d, slot), :], ret.at[rows_at(s, slot), :], rs.at[k], rr.at[k], (d, t)
        )
    ret[rows_at(s, slot), :] = outr[rows_at(s, slot), :]

    for k in late:
        forward(0, k)
    for k in near + late:
        forward(1, k)

    rc(nq(t_core), nq(t_core), n2s.at[1], n2r.at[1], (s, t_core)).wait_recv()
    rc(nq(t_far), nq(t_far), n2s.at[2], n2r.at[2], (s, t_core)).wait_recv()

    width = qg_ref.shape[1]

    def term(o):
        return mm(nall[o], gcall[o, :, :width], TN)

    acc = term(s)
    for k in near + late:
        acc = acc + term(z_from(k))

    for k in range(1, S):
        o = seq_from(k)
        rc(
            outr.at[rows_at(o, slot), :], ret.at[rows_at(o, slot), :], rs.at[k], rr.at[k], (o, t)
        ).wait_recv()
    pg_ref[...] = mm(ret[...], sel4, TN).astype(BF)

    for k in [0] + near + late:
        src = z_from(k) + 1 - 2 * y
        for e in range(2):
            rc(gpart(src, e), gpart(src, e), gys.at[e, k], gyr.at[e, k], (s_y, t)).wait_recv()
        acc = acc + term(src)
    qg_ref[...] = acc * (rows * S) ** (-0.5)
    for c in pending:
        c.wait_send()


def fused(S, T, patches, grad_merged, norm_gain, qkv_weight, proj_weight, grid_height, grid_width):
    rows, feat = grad_merged.shape
    cols = qkv_weight.shape[1]
    slot = rows // S
    quart = rows // T
    nslice = T * feat // S
    lanes = feat // 128 * 128 + 128
    Z = S // 2
    vm, sem = pltpu.VMEM, pltpu.SemaphoreType.DMA
    patch_t, qkv_grad = pl.pallas_call(
        functools.partial(kernel, S, T),
        out_shape=(
            jax.ShapeDtypeStruct((feat, 4 * rows), BF),
            jax.ShapeDtypeStruct((nslice, cols), F32),
        ),
        in_specs=[pl.BlockSpec(memory_space=pltpu.SMEM)] * 2
        + [pl.BlockSpec(memory_space=pltpu.VMEM)]
        + [pl.BlockSpec(memory_space=pl.ANY)] * 4,
        out_specs=[pl.BlockSpec(memory_space=pltpu.VMEM)] * 2,
        scratch_shapes=[
            vm((feat, 4 * rows), BF),
            vm((feat, rows), BF),
            vm((cols, T * feat), BF),
            vm(proj_weight.shape, BF),
            vm((2, rows, feat), BF),
            vm((T, 2, rows, feat), BF),
            vm((rows, T * feat), F32),
            vm((S, quart, nslice), BF),
            vm((S, rows, nslice), BF),
            vm((S, rows, -(-cols // 128) * 128), BF),
            vm((T, rows, lanes), BF),
            vm((T - 1, rows, lanes), BF),
            vm((rows, feat), BF),
            vm((rows, feat), BF),
            sem((4,)),
            sem((2, S)),
            sem((2, S)),
            sem((3, 2, 2)),
            sem((3, 2, 2)),
            sem((S,)),
            sem((S,)),
            sem((3,)),
            sem((3,)),
            sem((2, Z)),
            sem((2, Z)),
            sem((2, Z)),
            sem((2, Z)),
            sem((T - 1,)),
            sem((T - 1,)),
            sem((S,)),
            sem((S,)),
        ],
        compiler_params=pltpu.CompilerParams(
            collective_id=0, has_side_effects=True, vmem_limit_bytes=56 * 1024 * 1024
        ),
        cost_estimate=pl.CostEstimate(flops=1 << 30, bytes_accessed=5 << 20, transcendentals=1 << 16),
    )(
        grid_height,
        grid_width,
        norm_gain.reshape(1, T * feat),
        patches.T,
        grad_merged.T,
        qkv_weight.T,
        proj_weight,
    )
    return patch_t.T, qkv_grad


def solution(mesh):
    in_specs = (P("seq", "tp"), P("seq", "tp"), P(), P(None, "tp"), P("tp", None), P(), P())
    out_specs = (P("seq", "tp"), P("seq", "tp"))
    S, T = mesh.shape["seq"], mesh.shape["tp"]

    def body(*args):
        rows = args[1].shape[0]
        slot = rows // S
        if T == 4 and S % 2 == 0 and S <= 16 and rows % S == 0 and slot % 16 == 0:
            return fused(S, T, *args)
        return on_device(*args)

    return jax.shard_map(body, mesh=mesh, in_specs=in_specs, out_specs=out_specs, check_vma=False)
```

```python
import functools

import jax
import jax.numpy as jnp
from jax import lax
from jax.experimental import pallas as pl
from jax.experimental.pallas import tpu as pltpu
from jax.sharding import PartitionSpec as P

HEAD_SIZE = 104


soft_cap = 5.0
norm_eps = 1e-06


def stream_bounds(grid_height, grid_width, shard_count):
    image_sizes = grid_height * grid_width
    image_ends = jnp.cumsum(image_sizes)
    image_shard = jnp.arange(image_sizes.shape[0], dtype=jnp.int32) // 3
    owner_ids = jnp.arange(shard_count, dtype=jnp.int32)
    shard_load = jnp.sum(
        jnp.where(image_shard[None, :] == owner_ids[:, None], image_sizes[None, :], 0), axis=1
    )
    first_row = jnp.sum(
        jnp.where(image_shard[None, :] < owner_ids[:, None], image_sizes[None, :], 0), axis=1
    )
    return (image_ends, first_row, shard_load)


def pooled(window_rows, feat_width):
    summed = window_rows.reshape(-1, 4, feat_width).astype(jnp.float32).sum(axis=1)
    return (summed * 0.25).astype(jnp.bfloat16)


def on_device(patches, grad_merged, norm_gain, qkv_weight, proj_weight, grid_height, grid_width):
    shard_count = lax.axis_size("seq")
    myself = lax.axis_index("seq")
    tp_index = lax.axis_index("tp")
    row_count = grad_merged.shape[0]
    feat_width = grad_merged.shape[1]
    slot_count = -(-row_count // shard_count)
    slot_total = shard_count * slot_count
    image_ends, first_row, shard_load = stream_bounds(grid_height, grid_width, shard_count)
    stream_total = image_ends[-1]
    slot_ids = jnp.arange(slot_count, dtype=jnp.int32)
    owner_ids = jnp.arange(shard_count, dtype=jnp.int32)
    lead_row = (first_row - myself + shard_count - 1) // shard_count
    placed = lead_row[:, None] + slot_ids[None, :]
    sending = (placed * shard_count + myself < (first_row + shard_load)[:, None]) & (
        placed < row_count
    )
    picked = jnp.minimum(placed, row_count - 1).reshape(-1)

    def outgoing(source_rows):
        chosen = source_rows[picked].reshape(shard_count, slot_count, source_rows.shape[1])
        return jnp.where(sending[:, :, None], chosen, 0)

    windows = patches.reshape(row_count, 4 * feat_width)
    arrived_win, arrived_grad = (
        lax.all_to_all(outgoing(windows), "seq", split_axis=0, concat_axis=0, tiled=True),
        lax.all_to_all(outgoing(grad_merged), "seq", split_axis=0, concat_axis=0, tiled=True),
    )
    arrived = pooled(arrived_win.reshape(slot_total, 4 * feat_width), feat_width)
    arrived_grad = arrived_grad.reshape(slot_total, feat_width)
    row_values, row_grads = (
        lax.all_gather(arrived, "tp", axis=1, tiled=True),
        lax.all_gather(arrived_grad, "tp", axis=1, tiled=True),
    )
    first_here = first_row[myself]
    end_here = first_here + shard_load[myself]
    stream_in = (
        ((first_here - owner_ids + shard_count - 1) // shard_count)[:, None] + slot_ids[None, :]
    ) * shard_count + owner_ids[:, None]
    stream_in = stream_in.reshape(-1)
    live = stream_in < end_here
    image_index = jnp.sum(image_ends[None, :] <= stream_in[:, None], axis=1)
    image_key = jnp.where(live, image_index, -1 - jnp.arange(slot_total, dtype=jnp.int32))
    same_image = image_key[:, None] == image_key[None, :]
    values_f32 = row_values.astype(jnp.float32)
    inv_rms = lax.rsqrt(jnp.mean(values_f32 * values_f32, axis=-1, keepdims=True) + norm_eps)
    unit_rows = values_f32 * inv_rms
    normed = (unit_rows * norm_gain).astype(jnp.bfloat16)
    head_count = qkv_weight.shape[1] // (3 * HEAD_SIZE)
    packed = jnp.dot(normed, qkv_weight, preferred_element_type=jnp.float32).astype(jnp.bfloat16)
    packed = packed.reshape(slot_total, head_count, 3, HEAD_SIZE)
    queries = packed[:, :, 0]
    key_rows = packed[:, :, 1]
    values = packed[:, :, 2]
    score_scale = HEAD_SIZE ** (-0.5)
    logits = (
        jnp.einsum("qhe,khe->hqk", queries, key_rows, preferred_element_type=jnp.float32)
        * score_scale
    )
    capped = jnp.tanh(logits * (1.0 / soft_cap))
    raised = jnp.where(same_image[None], jnp.exp(soft_cap * capped), 0.0)
    attn_probs = raised / jnp.sum(raised, axis=-1, keepdims=True)
    probs_half = attn_probs.astype(jnp.bfloat16)
    grad_heads = jnp.einsum(
        "rd,cd->rc", row_grads, proj_weight, preferred_element_type=jnp.float32
    ).astype(jnp.bfloat16)
    grad_heads = grad_heads.reshape(slot_total, head_count, HEAD_SIZE)
    grad_prob = jnp.einsum("qhe,khe->hqk", grad_heads, values, preferred_element_type=jnp.float32)
    grad_score = attn_probs * (grad_prob - jnp.sum(attn_probs * grad_prob, axis=-1, keepdims=True))
    grad_logit = (grad_score * (1.0 - capped * capped)).astype(jnp.bfloat16)
    grad_query = (
        jnp.einsum("hqk,khe->qhe", grad_logit, key_rows, preferred_element_type=jnp.float32)
        * score_scale
    ).astype(jnp.bfloat16)
    grad_key = (
        jnp.einsum("hqk,qhe->khe", grad_logit, queries, preferred_element_type=jnp.float32)
        * score_scale
    ).astype(jnp.bfloat16)
    grad_value = jnp.einsum(
        "hqk,qhe->khe", probs_half, grad_heads, preferred_element_type=jnp.float32
    ).astype(jnp.bfloat16)
    grad_cols = jnp.stack([grad_query, grad_key, grad_value], axis=2).reshape(
        slot_total, 3 * head_count * HEAD_SIZE
    )
    head_part = jnp.einsum("rc,dc->rd", grad_cols, qkv_weight, preferred_element_type=jnp.float32)
    grad_normed = lax.psum(head_part, "tp")
    scaled = grad_normed * norm_gain
    grad_rows = inv_rms * (
        scaled - unit_rows * jnp.mean(scaled * unit_rows, axis=-1, keepdims=True)
    ) + row_grads.astype(jnp.float32)
    grad_rows = jnp.where(live[:, None], grad_rows, 0.0).astype(jnp.bfloat16)
    own_cols = lax.dynamic_slice_in_dim(grad_rows, tp_index * feat_width, feat_width, 1)
    local_rows = jnp.arange(row_count, dtype=jnp.int32)
    stream_out = local_rows * shard_count + myself
    owner_of = jnp.sum((first_row + shard_load)[None, :] <= stream_out[:, None], axis=1)
    owner_safe = jnp.minimum(owner_of, shard_count - 1)
    valid_out = stream_out < stream_total
    flat_out = jnp.clip(
        owner_safe * slot_count + local_rows - lead_row[owner_safe], 0, slot_total - 1
    )
    quarter = jnp.broadcast_to((own_cols * 0.25)[:, None, :], (slot_total, 4, feat_width))
    returned = lax.all_to_all(
        quarter.reshape(shard_count, slot_count, 4 * feat_width),
        "seq",
        split_axis=0,
        concat_axis=0,
        tiled=True,
    )
    windows_back = returned.reshape(slot_total, 4 * feat_width)[flat_out]
    windows_back = jnp.where(valid_out[:, None], windows_back, 0)
    patch_grad = windows_back.reshape(4 * row_count, feat_width)
    qkv_sum = lax.psum_scatter(
        jnp.einsum("rd,rc->dc", normed, grad_cols, preferred_element_type=jnp.float32),
        "seq",
        scatter_dimension=0,
        tiled=True,
    )
    qkv_grad = qkv_sum * (row_count * shard_count) ** (-0.5)
    return (patch_grad, qkv_grad)


MESH = pl.DeviceIdType.MESH
NT = (((1,), (1,)), ((), ()))
TN = (((0,), (0,)), ((), ()))
BF = jnp.bfloat16
F32 = jnp.float32


def mm(a, b, dims=(((1,), (0,)), ((), ()))):
    return lax.dot_general(a, b, dims, preferred_element_type=F32)


def kernel(
    S,
    T,
    gh_ref,
    gw_ref,
    gain_ref,
    patches_hbm,
    grads_hbm,
    w_hbm,
    proj_hbm,
    pg_ref,
    qg_ref,
    patches,
    grads,
    w,
    proj,
    picked,
    xg,
    nrmf,
    nst,
    nall,
    gcall,
    hps,
    hpr,
    hsum,
    outr,
    ret,
    load_sem,
    s1s,
    s1r,
    s2s,
    s2r,
    n1s,
    n1r,
    n2s,
    n2r,
    gzs,
    gzr,
    gys,
    gyr,
    hs,
    hr,
    rs,
    rr,
):
    s = lax.axis_index("seq")
    t = lax.axis_index("tp")
    feat, rows = grads.shape
    half = S // 2
    slot = rows // S
    quart = rows // T
    wide = T * feat
    nslice = wide // S
    per_block = S // T
    Z = S // 2
    z = s // 2
    y = lax.rem(s, 2)
    t_core = t + 1 - 2 * lax.rem(t, 2)
    t_x = lax.rem(t + 2, T)
    t_far = t_core + 2 - 4 * (t_core // 2)
    s_y = s + 1 - 2 * y

    loads = [
        pltpu.make_async_copy(a, b, load_sem.at[i])
        for i, (a, b) in enumerate(
            ((patches_hbm, patches), (grads_hbm, grads), (w_hbm, w), (proj_hbm, proj))
        )
    ]
    for c in loads:
        c.start()

    def seq_peer(k):
        return lax.rem(s + k, S)

    def seq_from(k):
        return lax.rem(s + S - k, S)

    barrier = pltpu.get_barrier_semaphore()
    for k in range(1, S):
        pl.semaphore_signal(barrier, inc=1, device_id=(seq_peer(k), t), device_id_type=MESH)
    for k in range(1, T):
        pl.semaphore_signal(barrier, inc=1, device_id=(s, lax.rem(t + k, T)), device_id_type=MESH)

    starts = []
    total = jnp.int32(0)
    first_here = jnp.int32(0)
    sizes = []
    for i in range(3 * S):
        if i % 3 == 0:
            starts.append(total)
            first_here = jnp.where(s == i // 3, total, first_here)
        size = gh_ref[i] * gw_ref[i]
        sizes.append(size)
        total = total + size
    starts.append(total)
    end0 = first_here
    end1 = first_here
    end2 = first_here
    for d in range(S):
        here = s == d
        end0 = jnp.where(here, starts[d] + sizes[3 * d], end0)
        end1 = jnp.where(here, starts[d] + sizes[3 * d] + sizes[3 * d + 1], end1)
        end2 = jnp.where(here, starts[d + 1], end2)

    def local_row(shape, dim):
        r = lax.broadcasted_iota(jnp.int32, shape, dim)
        d_of = r // slot
        j = r - d_of * slot
        lead = jnp.zeros(shape, jnp.int32)
        end = jnp.zeros(shape, jnp.int32)
        for d in range(S):
            lead = jnp.where(d_of == d, (starts[d] - s + S - 1) // S, lead)
            end = jnp.where(d_of == d, starts[d + 1], end)
        row = lead + j
        return jnp.where((row * S + s < end) & (row < rows), row, -1)

    def arrival(shape, dim):
        r = lax.broadcasted_iota(jnp.int32, shape, dim)
        o = r // slot
        j = r - o * slot
        g = ((first_here - o + S - 1) // S + j) * S + o
        alive = g < end2
        key = jnp.where(g >= end0, 1, 0) + jnp.where(g >= end1, 1, 0)
        return jnp.where(alive, key, 3 + r), alive

    lrow = local_row((rows, 1), 0)
    sel4 = jnp.where(
        lax.broadcasted_iota(jnp.int32, (rows, 4 * rows), 1) // 4 == lrow, 0.25, 0.0
    ).astype(BF)
    sel1 = jnp.where(lax.broadcasted_iota(jnp.int32, (rows, rows), 1) == lrow, 1.0, 0.0).astype(BF)
    loads[0].wait()
    picked[0] = mm(sel4, patches[...], NT).astype(BF)
    loads[1].wait()
    picked[1] = mm(sel1, grads[...], NT).astype(BF)

    pl.semaphore_wait(barrier, S + T - 2)

    def rc(src, dst, ss, rsem, dev):
        return pltpu.make_async_remote_copy(
            src_ref=src,
            dst_ref=dst,
            send_sem=ss,
            recv_sem=rsem,
            device_id=dev,
            device_id_type=MESH,
        )

    def rows_at(i, n):
        return pl.ds(pl.multiple_of(i * n, n), n)

    pending = []

    def send(*a):
        c = rc(*a)
        c.start()
        pending.append(c)

    side = s // half
    place = lax.rem(s, half)

    def group(g):
        return side if g == 0 else 1 - side

    def s1_peer(g, k):
        return group(g) * half + lax.rem(place + k, half)

    def s1_from(g, k):
        return group(g) * half + lax.rem(place + half - k, half)

    def xrows(b, i, g):
        return xg.at[b, i, rows_at(group(g), half * slot), :]

    for i in range(2):
        for g in range(2):
            for k in range(1 - g, half):
                d = s1_peer(g, k)
                send(
                    picked.at[i, rows_at(d, slot), :],
                    xg.at[t, i, rows_at(s, slot), :],
                    s1s.at[i, g * half + k],
                    s1r.at[i, g * half + k],
                    (d, t),
                )
    xg[t, :, rows_at(s, slot), :] = picked[:, rows_at(s, slot), :]
    key_r, live = arrival((rows, 1), 0)
    key_c, _ = arrival((1, rows), 1)
    same = key_r == key_c

    def pass_on(i, g):
        for k in range(1 - g, half):
            o = s1_from(g, k)
            rc(
                picked.at[i, rows_at(o, slot), :],
                xg.at[t, i, rows_at(o, slot), :],
                s1s.at[i, g * half + k],
                s1r.at[i, g * half + k],
                (o, t),
            ).wait_recv()
        send(xrows(t, i, g), xrows(t, i, g), s2s.at[0, i, g], s2r.at[0, i, g], (s, t_x))
        send(xrows(t, i, g), xrows(t, i, g), s2s.at[1, i, g], s2r.at[1, i, g], (s, t_core))

    def relay(i, g):
        block = xrows(t_x, i, g)
        rc(block, block, s2s.at[0, i, g], s2r.at[0, i, g], (s, t_x)).wait_recv()
        send(block, block, s2s.at[2, i, g], s2r.at[2, i, g], (s, t_core))

    def wait_rest(i):
        for g in range(2):
            for j, b in ((1, t_core), (2, t_far)):
                block = xrows(b, i, g)
                rc(block, block, s2s.at[j, i, g], s2r.at[j, i, g], (s, t_core)).wait_recv()

    def all_features(i):
        return jnp.concatenate([xg[b, i].astype(F32) for b in range(T)], axis=1)

    pass_on(0, 0)
    pass_on(0, 1)
    pass_on(1, 0)
    relay(0, 0)
    pass_on(1, 1)
    relay(0, 1)
    wait_rest(0)
    gain = gain_ref[...].reshape(1, wide)
    x_all = all_features(0)
    inv = lax.rsqrt(jnp.sum(x_all * x_all, axis=1, keepdims=True) * (1.0 / wide) + norm_eps)
    normed_f = x_all * inv * gain
    nrmf[...] = normed_f
    normed = normed_f.astype(BF)
    part = nrmf[rows_at(t, quart), :]
    for d in range(S):
        nst[d] = part[:, d * nslice : (d + 1) * nslice].astype(BF)
    for k in range(1, S):
        d = seq_peer(k)
        send(nst.at[d], nall.at[s, rows_at(t, quart), :], n1s.at[k], n1r.at[k], (d, t))
    nall[s, rows_at(t, quart), :] = nst[s]
    relay(1, 0)
    relay(1, 1)

    loads[2].wait()
    packed = mm(w[...], normed, NT)
    loads[3].wait()
    wait_rest(1)
    heads_grad = mm(proj[...], all_features(1).astype(BF), NT)

    head_count = w.shape[0] // (3 * HEAD_SIZE)
    scale = HEAD_SIZE ** (-0.5)
    cols = []
    early = 3 * HEAD_SIZE // 16 * 16
    near = [1, Z - 1] if Z > 2 else [1]
    late = list(range(2, Z - 1))

    def gpart(o, e):
        return gcall.at[o, pl.ds(0, early) if e == 0 else pl.ds(early, gcall.shape[1] - early), :]

    def z_from(k):
        return 2 * lax.rem(z + Z - k, Z) + y

    def spread(e):
        block = gpart(s, e)
        for k in near + late:
            d = 2 * lax.rem(z + k, Z) + y
            send(block, block, gzs.at[e, k], gzr.at[e, k], (d, t))
        send(block, block, gys.at[e, 0], gyr.at[e, 0], (s_y, t))

    def forward(e, k):
        block = gpart(z_from(k), e)
        rc(block, block, gzs.at[e, k], gzr.at[e, k], (z_from(k), t)).wait_recv()
        send(block, block, gys.at[e, k], gyr.at[e, k], (s_y, t))

    def nq(b):
        return nall.at[:, rows_at(b, quart), :]

    for h in range(head_count):
        q, kk, v = (
            packed[(3 * h + i) * HEAD_SIZE : (3 * h + i + 1) * HEAD_SIZE].astype(BF)
            for i in range(3)
        )
        gh = heads_grad[h * HEAD_SIZE : (h + 1) * HEAD_SIZE].astype(BF)
        capped = jnp.tanh(mm(q, kk, TN) * (scale / soft_cap))
        raised = jnp.where(same, jnp.exp(soft_cap * capped), 0.0)
        prob = raised / jnp.sum(raised, axis=1, keepdims=True)
        gp = mm(gh, v, TN)
        gs = prob * (gp - jnp.sum(prob * gp, axis=1, keepdims=True))
        gl = (gs * (1.0 - capped * capped)).astype(BF)
        cols.append(mm(kk, gl, NT) * scale)
        cols.append(mm(q, gl) * scale)
        cols.append(mm(gh, prob.astype(BF)))
        if h == 0:
            gcall[s, :early, :] = jnp.concatenate(cols, axis=0)[:early].astype(BF)
            spread(0)
    grad_f = jnp.concatenate(cols, axis=0)
    grad_cols = grad_f.astype(BF)
    gcall[s, early:, :] = grad_cols[early:]
    spread(1)

    product = (grad_cols.astype(F32) * packed).astype(BF)
    dot_tile = mm(product, jnp.ones((product.shape[0], hps.shape[2] - feat), BF), TN)
    row_dot = dot_tile[:, :1]
    every = mm(grad_cols, w[...], TN)
    own_part = jnp.zeros((rows, feat), F32)
    gain_own = jnp.zeros((1, feat), F32)
    across = jnp.zeros((rows, hps.shape[2]), F32)
    for b in range(T):
        part = every[:, b * feat : (b + 1) * feat]
        block = jnp.concatenate([part, dot_tile], axis=1)
        hps[b] = block.astype(BF)
        across = jnp.where(t_x == b, block, across)
        own_part = jnp.where(t == b, part, own_part)
        gain_own = jnp.where(t == b, gain[:, b * feat : (b + 1) * feat], gain_own)
    send(hps.at[t_far], hpr.at[1], hs.at[1], hr.at[1], (s, t_core))
    send(hps.at[t_core], hpr.at[0], hs.at[0], hr.at[0], (s, t_core))
    rc(hps.at[t_far], hpr.at[1], hs.at[1], hr.at[1], (s, t_core)).wait_recv()
    hsum[...] = (across + hpr[1].astype(F32)).astype(BF)
    send(hsum, hpr.at[2], hs.at[2], hr.at[2], (s, t_x))

    for k in range(1, S):
        o = seq_from(k)
        rc(nst.at[o], nall.at[o, rows_at(t, quart), :], n1s.at[k], n1r.at[k], (o, t)).wait_recv()
    send(nq(t), nq(t), n2s.at[0], n2r.at[0], (s, t_x))
    send(nq(t), nq(t), n2s.at[1], n2r.at[1], (s, t_core))
    for k in near:
        forward(0, k)

    for i, b in ((0, t_core), (2, t_x)):
        rc(hsum, hpr.at[i], hs.at[i], hr.at[i], (s, b)).wait_recv()
        came = hpr[i].astype(F32)
        own_part = own_part + came[:, :feat]
        row_dot = row_dot + came[:, feat : feat + 1]
    scaled = own_part * gain_own
    mean = row_dot * (1.0 / wide)
    unit = xg[t, 0].astype(F32) * inv
    grad_rows = inv * (scaled - unit * mean) + xg[t, 1].astype(F32)
    outr[...] = jnp.where(live, grad_rows, 0.0).astype(BF)
    for k in range(1, S):
        d = seq_peer(k)
        send(
            outr.at[rows_at(d, slot), :], ret.at[rows_at(s, slot), :], rs.at[k], rr.at[k], (d, t)
        )
    ret[rows_at(s, slot), :] = outr[rows_at(s, slot), :]

    for k in late:
        forward(0, k)
    for k in near:
        forward(1, k)
    rc(nq(t_x), nq(t_x), n2s.at[0], n2r.at[0], (s, t_x)).wait_recv()
    send(nq(t_x), nq(t_x), n2s.at[2], n2r.at[2], (s, t_core))
    for k in late:
        forward(1, k)

    rc(nq(t_core), nq(t_core), n2s.at[1], n2r.at[1], (s, t_core)).wait_recv()
    rc(nq(t_far), nq(t_far), n2s.at[2], n2r.at[2], (s, t_core)).wait_recv()

    def term(o):
        return mm(gcall[o], nall[o])

    acc = term(s)
    for k in near + late:
        acc = acc + term(z_from(k))

    for k in range(1, S):
        o = seq_from(k)
        rc(
            outr.at[rows_at(o, slot), :], ret.at[rows_at(o, slot), :], rs.at[k], rr.at[k], (o, t)
        ).wait_recv()
    pg_ref[...] = mm(ret[...], sel4, TN).astype(BF)

    for k in [0] + near + late:
        src = z_from(k) + 1 - 2 * y
        for e in range(2):
            rc(gpart(src, e), gpart(src, e), gys.at[e, k], gyr.at[e, k], (s_y, t)).wait_recv()
        acc = acc + term(src)
    qg_ref[...] = acc * (rows * S) ** (-0.5)
    for c in pending:
        c.wait_send()


def fused(S, T, patches, grad_merged, norm_gain, qkv_weight, proj_weight, grid_height, grid_width):
    rows, feat = grad_merged.shape
    cols = qkv_weight.shape[1]
    slot = rows // S
    quart = rows // T
    nslice = T * feat // S
    lanes = feat // 128 * 128 + 128
    Z = S // 2
    vm, sem = pltpu.VMEM, pltpu.SemaphoreType.DMA
    patch_t, grad_t = pl.pallas_call(
        functools.partial(kernel, S, T),
        out_shape=(
            jax.ShapeDtypeStruct((feat, 4 * rows), BF),
            jax.ShapeDtypeStruct((cols, nslice), F32),
        ),
        in_specs=[pl.BlockSpec(memory_space=pltpu.SMEM)] * 2
        + [pl.BlockSpec(memory_space=pltpu.VMEM)]
        + [pl.BlockSpec(memory_space=pl.ANY)] * 4,
        out_specs=[pl.BlockSpec(memory_space=pltpu.VMEM)] * 2,
        scratch_shapes=[
            vm((feat, 4 * rows), BF),
            vm((feat, rows), BF),
            vm((cols, T * feat), BF),
            vm(proj_weight.shape, BF),
            vm((2, rows, feat), BF),
            vm((T, 2, rows, feat), BF),
            vm((rows, T * feat), F32),
            vm((S, quart, nslice), BF),
            vm((S, rows, nslice), BF),
            vm((S, cols, rows), BF),
            vm((T, rows, lanes), BF),
            vm((T - 1, rows, lanes), BF),
            vm((rows, lanes), BF),
            vm((rows, feat), BF),
            vm((rows, feat), BF),
            sem((4,)),
            sem((2, S)),
            sem((2, S)),
            sem((3, 2, 2)),
            sem((3, 2, 2)),
            sem((S,)),
            sem((S,)),
            sem((3,)),
            sem((3,)),
            sem((2, Z)),
            sem((2, Z)),
            sem((2, Z)),
            sem((2, Z)),
            sem((T - 1,)),
            sem((T - 1,)),
            sem((S,)),
            sem((S,)),
        ],
        compiler_params=pltpu.CompilerParams(
            collective_id=0, has_side_effects=True, vmem_limit_bytes=56 * 1024 * 1024
        ),
        cost_estimate=pl.CostEstimate(flops=1 << 30, bytes_accessed=5 << 20, transcendentals=1 << 16),
    )(
        grid_height,
        grid_width,
        norm_gain,
        patches.T,
        grad_merged.T,
        qkv_weight.T,
        proj_weight,
    )
    return patch_t.T, grad_t.T


def solution(mesh):
    in_specs = (P("seq", "tp"), P("seq", "tp"), P(), P(None, "tp"), P("tp", None), P(), P())
    out_specs = (P("seq", "tp"), P("seq", "tp"))
    S, T = mesh.shape["seq"], mesh.shape["tp"]

    def body(*args):
        rows = args[1].shape[0]
        slot = rows // S
        if T == 4 and S % 2 == 0 and S <= 16 and rows % S == 0 and slot % 16 == 0:
            return fused(S, T, *args)
        return on_device(*args)

    return jax.shard_map(body, mesh=mesh, in_specs=in_specs, out_specs=out_specs, check_vma=False)
```
